256 devices in a mesh: replica: 16 (over z, y_lo), fsdp: 16 (over y_hi, x, core).
Axes of the slice: x: 4, y: 4 (y_hi: 2, y_lo: 2; y = y_hi * 2 + y_lo), z: 8, core: 2. Of those that a mesh axis runs over, the one named last changes fastest.
Arguments:
- tokens: bfloat16 [16, 8192, 4608], P('replica', 'fsdp'), may hold values from -6 to 6
- targets: bfloat16 [16, 8192, 1024], P('replica', 'fsdp'), may hold values from -6 to 6
- local_weights: bfloat16 [16, 4608, 1024], P('replica', 'fsdp'), may hold values from -5 to 5, as said below
- first_moment: float32 [16, 4608, 1024], P('replica', 'fsdp'), may hold values from -6 to 6
- second_moment: float32 [16, 4608, 1024], P('replica', 'fsdp'), may hold values from 0.5 to 4
- global_weights: float32 [4608, 1024], P('fsdp'), may hold values from -4 to 4
- outer_momentum: float32 [4608, 1024], P('fsdp'), may hold values from -0.6 to 0.6
Outputs:
- new_local: bfloat16 [16, 4608, 1024], P('replica', 'fsdp')
- new_first: float32 [16, 4608, 1024], P('replica', 'fsdp')
- new_second: float32 [16, 4608, 1024], P('replica', 'fsdp')
- new_global: float32 [4608, 1024], P('fsdp')
- new_momentum: float32 [4608, 1024], P('fsdp')
The draws below stay inside these ranges and needn't reach their ends.
Inputs may be any that keep to these rules, and one draw needn't show every extreme that they name: `local_weights`: each replica's weights lie near global_weights.
All inputs are finite; a program needn't handle non-finite values.
Results may differ from the reference program's by a relative error of at most 0.024.
Values may be sent and summed in bfloat16 or wider, within the bound.
No kernel may reach another device: no remote copies, remote signals or barrier semaphores. Data moves between devices by JAX's collectives and lax.ppermute only.
A program may use at most 128 MiB of HBM per device.

```python
import math
import jax
import jax.numpy as jnp
from jax import lax

D = 4608
KVW = 1024
TOK_DEV = 512
INNER = 1
ROWS = 8192
REPLICAS = 16
N_FSDP = 16


def shared_base(key):
    return jnp.clip(jax.random.normal(key, (D, KVW), jnp.float32), -4.0, 4.0)


def draw_global_weights(key, part):
    return shared_base(key)


def draw_local_weights(key, part):
    base = shared_base(key)
    key = jax.random.fold_in(key, 7)
    noise = jax.random.normal(key, (REPLICAS, D, KVW), jnp.float32)
    return jnp.clip(base[None] + 0.25 * noise, -5.0, 5.0).astype(jnp.bfloat16)


def shard_levels(rng, extent, shards, least, largest):
    gain = 1.0
    for dim, shards_of in shards:
        draws = jax.random.uniform(jax.random.fold_in(jax.random.fold_in(rng, 6), dim), (shards_of,), jnp.float32, least / len(shards), largest / len(shards))
        gain = gain * jnp.repeat(jnp.exp(draws), extent[dim] // shards_of).reshape((-1,) + (1,) * (len(extent) - 1 - dim))
    return gain


def scatter_about(own_key, dims, scale, reach, pieces=(), kind=jnp.bfloat16):
    entries = jax.random.normal(own_key, dims, jnp.float32) * scale
    if len(pieces) > 0:
        entries = shard_levels(own_key, dims, pieces, -0.22, 0.18) * entries
    return jnp.clip(entries, min=-reach, max=reach).astype(kind)


def setup_inputs(seed: int = 0) -> dict:
    splits = jax.random.split(jax.random.key(seed), 8)
    return {
        "tokens": scatter_about(splits[0], (REPLICAS, ROWS, D), 1.0, 6.0, ((0, 16), (1, 16))),
        "targets": scatter_about(splits[1], (REPLICAS, ROWS, KVW), 1.0, 6.0, ((0, 16), (1, 16))),
        "local_weights": draw_local_weights(jax.random.fold_in(splits[7], 71), 0),
        "first_moment": scatter_about(splits[3], (REPLICAS, D, KVW), 1.0, 6.0, ((0, 16), (1, 16)), jnp.float32),
        "second_moment": jnp.clip(jnp.exp(math.log(4.0) - 2.0794415 * jax.random.uniform(splits[4], (REPLICAS, D, KVW), jnp.float32) ** shard_levels(splits[4], (REPLICAS, D, KVW), ((0, 16), (1, 16)), -0.2, 0.2)), 0.5, 4.0),
        "global_weights": draw_global_weights(jax.random.fold_in(splits[7], 71), 0),
        "outer_momentum": scatter_about(splits[6], (D, KVW), 0.1, 0.6, ((0, 16),), jnp.float32),
    }


inner_rate = 0.02
first_decay = 0.5
second_decay = 0.95
adam_eps = 1e-08
weight_decay = 0.1
outer_rate = 0.7
outer_mu = 0.9
mix_keep = 0.5

def block_grad(rows, residual):
    row_blocks = rows.reshape(N_FSDP, TOK_DEV, D)
    res_blocks = residual.reshape(N_FSDP, TOK_DEV, KVW)

    def add_block(total, pair):
        block_rows, block_res = pair
        part = lax.dot_general(block_rows, block_res, (((0,), (0,)), ((), ())), preferred_element_type=jnp.float32)
        return (total + part.astype(jnp.bfloat16).astype(jnp.float32), None)
    total, unused = lax.scan(add_block, jnp.zeros((D, KVW), jnp.float32), (row_blocks, res_blocks))
    return total

def inner_steps(packed, global_weights):
    rows, wanted, weight, first, second = packed
    out_scale = 1.0 / math.sqrt(D)
    grad_scale = 1.0 / math.sqrt(ROWS)
    for step in range(INNER):
        projected = jnp.dot(rows, weight, preferred_element_type=jnp.float32) * out_scale
        residual = (projected - wanted.astype(jnp.float32)).astype(jnp.bfloat16)
        grad = block_grad(rows, residual) * grad_scale
        first = first_decay * first + (1.0 - first_decay) * grad
        second = second_decay * second + (1.0 - second_decay) * grad * grad
        wide = weight.astype(jnp.float32)
        weight = (wide - inner_rate * (first / (jnp.sqrt(second) + adam_eps) + weight_decay * wide)).astype(jnp.bfloat16)
    delta = (global_weights - weight.astype(jnp.float32)).astype(jnp.bfloat16)
    return (weight, first, second, delta)

def reference(tokens, targets, local_weights, first_moment, second_moment, global_weights, outer_momentum):
    weights, new_first, new_second, deltas = lax.map(lambda packed: inner_steps(packed, global_weights), (tokens, targets, local_weights, first_moment, second_moment))
    total = lax.optimization_barrier(jnp.sum(deltas.astype(jnp.float32), axis=0))
    mean = total / REPLICAS
    new_momentum = outer_mu * outer_momentum + mean
    new_global = global_weights - outer_rate * (mean + outer_mu * new_momentum)
    new_local = (mix_keep * weights.astype(jnp.float32) + (1.0 - mix_keep) * new_global[None]).astype(jnp.bfloat16)
    return (new_local, new_first, new_second, new_global, new_momentum)
```

```python
import math

import jax
import jax.numpy as jnp
from jax import lax
from jax.experimental import pallas as pl
from jax.experimental.pallas import tpu as pltpu
from jax.sharding import PartitionSpec as P

inner_rate = 0.02
first_decay = 0.5
second_decay = 0.95
adam_eps = 1e-08
weight_decay = 0.1
outer_rate = 0.7
outer_mu = 0.9
mix_keep = 0.5

BF = jnp.bfloat16
F32 = jnp.float32

D = 4608
KVW = 1024
TOK = 512
UNIT = 288
PART = 96
QUAD = 4 * PART
HALF = 2304
REPLICAS = 16
MIB = 1024 * 1024

EVEN, ODD, WIDE = 0, 1, 2
ORDERS = ((EVEN, ODD, WIDE), (ODD, WIDE, EVEN), (WIDE, EVEN, ODD))
FLIP = {EVEN: 2, ODD: 6, WIDE: 8}
SWAP_CORE = [(i, i ^ 1) for i in range(16)]


def chip_bit(chip, dim):
    x = chip % 4
    if dim == EVEN:
        return (x ^ (x // 2)) % 2
    if dim == ODD:
        return x // 2
    return chip // 4


def unit_order(part):
    one, two, three = ORDERS[part]
    return sorted(
        range(8), key=lambda chip: (chip_bit(chip, three), chip_bit(chip, two), chip_bit(chip, one))
    )


def own_bits():
    me = lax.axis_index("fsdp")
    x = (me >> 1) & 3
    return {EVEN: (x ^ (x >> 1)) & 1, ODD: x >> 1, WIDE: me >> 3}, me & 1


def flip(value, dim):
    return lax.ppermute(value, "fsdp", [(i, i ^ FLIP[dim]) for i in range(16)])


def swap(value):
    return lax.ppermute(value, "fsdp", SWAP_CORE)


def params(mib):
    return pltpu.CompilerParams(vmem_limit_bytes=mib * MIB)


def cost(flops, nbytes):
    return pl.CostEstimate(flops=flops, bytes_accessed=nbytes, transcendentals=0)


def pack_kernel(core_ref, rows_ref, keep_ref, send_ref):
    rows = rows_ref[...]

    def packed(core):
        pieces = []
        for part in range(3):
            for chip in unit_order(part):
                at = 2 * UNIT * chip + UNIT * core + PART * part
                pieces.append(rows[:, at : at + PART])
        return jnp.concatenate(pieces, axis=1)

    zero = packed(0)
    one = packed(1)

    @pl.when(core_ref[0] == 0)
    def _():
        keep_ref[...] = zero
        send_ref[...] = one

    @pl.when(core_ref[0] == 1)
    def _():
        keep_ref[...] = one
        send_ref[...] = zero


def pack(core, rows):
    tile = 128
    return pl.pallas_call(
        pack_kernel,
        grid_spec=pltpu.PrefetchScalarGridSpec(
            num_scalar_prefetch=1,
            grid=(TOK // tile,),
            in_specs=[pl.BlockSpec((tile, D), lambda i, s: (i, 0))],
            out_specs=[pl.BlockSpec((tile, HALF), lambda i, s: (i, 0))] * 2,
        ),
        out_shape=[jax.ShapeDtypeStruct((TOK, HALF), BF)] * 2,
        compiler_params=params(40),
        cost_estimate=cost(0, 4 * TOK * D),
        name="pack",
    )(core, rows)


def turn_kernel(rows_ref, out_ref):
    out_ref[...] = rows_ref[...].T


def turn(rows):
    tile = 384
    return pl.pallas_call(
        turn_kernel,
        grid=(HALF // tile,),
        in_specs=[pl.BlockSpec((TOK, tile), lambda i: (0, i))],
        out_specs=pl.BlockSpec((tile, TOK), lambda i: (i, 0)),
        out_shape=jax.ShapeDtypeStruct((HALF, TOK), BF),
        compiler_params=params(40),
        cost_estimate=cost(0, 4 * TOK * HALF),
        name="turn",
    )(rows)


def dot(a, b):
    return jnp.dot(a, b, preferred_element_type=F32)


def project_first_kernel(at_ref, a0, a1, a2, w0, w1, w2, out_ref):
    out_ref[...] = dot(a0[...], w0[...]) + dot(a1[...], w1[...]) + dot(a2[...], w2[...])


def project_last_kernel(at_ref, a0, a1, a2, w0, w1, w2, acc_ref, wide_ref, out_ref):
    total = acc_ref[...] + (
        dot(a0[...], w0[...]) + dot(a1[...], w1[...]) + dot(a2[...], w2[...])
    )
    total = total * (1.0 / math.sqrt(D))
    wide_ref[...] = total
    out_ref[...] = total.astype(BF)


def project(at, rows, quads, acc=None):
    tile = 128

    def piece(part):
        return pl.BlockSpec((tile, QUAD), lambda i, s: (i, s[part]))

    whole = pl.BlockSpec((QUAD, KVW), lambda i, s: (0, 0))
    row = pl.BlockSpec((tile, KVW), lambda i, s: (i, 0))
    wide = jax.ShapeDtypeStruct((TOK, KVW), F32)
    first = acc is None
    return pl.pallas_call(
        project_first_kernel if first else project_last_kernel,
        grid_spec=pltpu.PrefetchScalarGridSpec(
            num_scalar_prefetch=1,
            grid=(TOK // tile,),
            in_specs=[piece(0), piece(1), piece(2), whole, whole, whole] + ([] if first else [row]),
            out_specs=row if first else [row, row],
        ),
        out_shape=wide if first else [wide, jax.ShapeDtypeStruct((TOK, KVW), BF)],
        compiler_params=params(40),
        cost_estimate=cost(2 * TOK * KVW * 3 * QUAD, 7 * MIB),
        name="project_first" if first else "project_last",
    )(at, rows, rows, rows, *quads, *([] if first else [acc]))


def grad_kernel(at_ref, a_ref, b_ref, ra_ref, rb_ref, out_ref):
    out_ref[...] = (dot(a_ref[...], ra_ref[...]) + dot(b_ref[...], rb_ref[...])).astype(
        out_ref.dtype
    )


def grad_block(at, turned, residuals, dtype):
    tile = 192
    steps = QUAD // tile
    piece = pl.BlockSpec((tile, TOK), lambda i, s: (s[0] * steps + i, 0))
    whole = pl.BlockSpec((TOK, KVW), lambda i, s: (0, 0))
    return pl.pallas_call(
        grad_kernel,
        grid_spec=pltpu.PrefetchScalarGridSpec(
            num_scalar_prefetch=1,
            grid=(steps,),
            in_specs=[piece, piece, whole, whole],
            out_specs=pl.BlockSpec((tile, KVW), lambda i, s: (i, 0)),
        ),
        out_shape=jax.ShapeDtypeStruct((QUAD, KVW), dtype),
        compiler_params=params(40),
        cost_estimate=cost(4 * QUAD * KVW * TOK, 4 * MIB),
        name="grad",
    )(at, *turned, *residuals)


def inner_kernel(grad_ref, w_ref, m_ref, v_ref, g_ref, m_out, v_out, w_out, delta_out):
    grad = grad_ref[...] * (1.0 / math.sqrt(TOK * 16))
    first = first_decay * m_ref[...] + (1.0 - first_decay) * grad
    second = second_decay * v_ref[...] + (1.0 - second_decay) * grad * grad
    m_out[...] = first
    v_out[...] = second
    wide = w_ref[...].astype(F32)
    weight = (
        wide - inner_rate * (first / (jnp.sqrt(second) + adam_eps) + weight_decay * wide)
    ).astype(BF)
    w_out[...] = weight
    delta = (g_ref[...] - weight.astype(F32)).astype(BF)
    for group in range(8):
        delta_out[group] = delta[:, 128 * group : 128 * group + 128]


def inner(grad, weight, first, second, base):
    row = pl.BlockSpec((PART, KVW), lambda i: (i, 0))
    wide = jax.ShapeDtypeStruct((UNIT, KVW), F32)
    return pl.pallas_call(
        inner_kernel,
        grid=(3,),
        in_specs=[row] * 5,
        out_specs=[row, row, row, pl.BlockSpec((8, PART, 128), lambda i: (0, i, 0))],
        out_shape=[
            wide,
            wide,
            jax.ShapeDtypeStruct((UNIT, KVW), BF),
            jax.ShapeDtypeStruct((8, UNIT, 128), BF),
        ],
        compiler_params=params(40),
        cost_estimate=cost(20 * UNIT * KVW, 9 * MIB),
        name="inner",
    )(grad, weight, first, second, base)


def total_kernel(parts_ref, out_ref):
    total = jnp.sum(parts_ref[...].astype(F32), axis=0)
    mean = (total * (1.0 / REPLICAS)).astype(BF)
    out_ref[...] = jnp.broadcast_to(mean[None], out_ref.shape)


def totals(parts):
    return pl.pallas_call(
        total_kernel,
        out_shape=jax.ShapeDtypeStruct(parts.shape, BF),
        compiler_params=params(40),
        cost_estimate=cost(0, 2 * MIB),
        name="totals",
    )(parts)


def outer_kernel(mean_ref, w_ref, g_ref, o_ref, local_out, global_out, momentum_out):
    mean = jnp.concatenate([mean_ref[group] for group in range(8)], axis=1).astype(F32)
    momentum = outer_mu * o_ref[...] + mean
    base = g_ref[...] - outer_rate * (mean + outer_mu * momentum)
    momentum_out[...] = momentum
    global_out[...] = base
    local_out[...] = (mix_keep * w_ref[...].astype(F32) + (1.0 - mix_keep) * base).astype(BF)


def outer(mean, weight, base, momentum):
    row = pl.BlockSpec((PART, KVW), lambda i: (i, 0))
    wide = jax.ShapeDtypeStruct((UNIT, KVW), F32)
    return pl.pallas_call(
        outer_kernel,
        grid=(3,),
        in_specs=[pl.BlockSpec((8, PART, 128), lambda i: (0, i, 0)), row, row, row],
        out_specs=[row, row, row],
        out_shape=[jax.ShapeDtypeStruct((UNIT, KVW), BF), wide, wide],
        compiler_params=params(40),
        cost_estimate=cost(8 * UNIT * KVW, 7 * MIB),
        name="outer",
    )(mean, weight, base, momentum)


def ordered(bit, own, other):
    size = own.shape[0]
    out = jnp.zeros((2 * size,) + own.shape[1:], own.dtype)
    out = lax.dynamic_update_slice(out, own, (bit * size, 0))
    return lax.dynamic_update_slice(out, other, ((1 - bit) * size, 0))


def half_at(value, index):
    size = value.shape[0] // 2
    return lax.dynamic_slice(value, (index * size, 0), (size, value.shape[1]))


def local(
    tokens, targets, local_weights, first_moment, second_moment, global_weights, outer_momentum
):
    rows = tokens[0]
    wanted = targets[0]
    weight = local_weights[0]
    bits, core = own_bits()
    core = core.astype(jnp.int32)
    quad_bits = [bits[ORDERS[part][2]] for part in range(3)]

    held = [weight[PART * part : PART * part + PART] for part in range(3)]
    for step in range(2):
        came = [flip(held[part], ORDERS[part][step]) for part in range(3)]
        held = [ordered(bits[ORDERS[part][step]], held[part], came[part]) for part in range(3)]
    far = [flip(held[part], ORDERS[part][2]) for part in range(3)]

    kept, sent = pack(core.reshape(1), rows)
    received = swap(sent)
    wanted_other = swap(wanted)
    near_at = jnp.stack([2 * part + quad_bits[part] for part in range(3)]).astype(jnp.int32)
    far_at = jnp.stack([2 * part + 1 - quad_bits[part] for part in range(3)]).astype(jnp.int32)
    turned = (turn(kept), turn(received))

    near_kept = project(near_at, kept, held)
    near_received = project(near_at, received, held)
    wide_kept, narrow_kept = project(far_at, kept, far, near_kept)
    cross_received = swap(narrow_kept)
    wide_received, narrow_received = project(far_at, received, far, near_received)
    cross_kept = swap(narrow_received)
    residuals = (
        (wide_kept + cross_kept.astype(F32) - wanted.astype(F32)).astype(BF),
        (wide_received + cross_received.astype(F32) - wanted_other.astype(F32)).astype(BF),
    )

    came = []
    for part in range(3):
        away = grad_block(far_at[part : part + 1], turned, residuals, BF)
        came.append(flip(away, ORDERS[part][2]))
    sums = []
    for part in range(3):
        stay = grad_block(near_at[part : part + 1], turned, residuals, F32)
        sums.append(stay + came[part].astype(F32))
    for step in (1, 0):
        away = []
        for part in range(3):
            bit = bits[ORDERS[part][step]]
            away.append(flip(half_at(sums[part], 1 - bit).astype(BF), ORDERS[part][step]))
        for part in range(3):
            bit = bits[ORDERS[part][step]]
            sums[part] = half_at(sums[part], bit) + away[part].astype(F32)
    grad = jnp.concatenate(sums, axis=0)

    first, second, weight, delta = inner(
        grad, weight, first_moment[0], second_moment[0], global_weights
    )
    pieces = lax.all_to_all(delta.reshape(REPLICAS, UNIT // 2, 128), "replica", 0, 0)
    mean = lax.all_to_all(totals(pieces), "replica", 0, 0).reshape(8, UNIT, 128)
    new_local, new_global, new_momentum = outer(mean, weight, global_weights, outer_momentum)
    return (new_local[None], first[None], second[None], new_global, new_momentum)


def solution(mesh):
    return jax.shard_map(
        local,
        mesh=mesh,
        in_specs=(
            P("replica", "fsdp", None),
            P("replica", "fsdp", None),
            P("replica", "fsdp", None),
            P("replica", "fsdp", None),
            P("replica", "fsdp", None),
            P("fsdp", None),
            P("fsdp", None),
        ),
        out_specs=(
            P("replica", "fsdp", None),
            P("replica", "fsdp", None),
            P("replica", "fsdp", None),
            P("fsdp", None),
            P("fsdp", None),
        ),
        check_vma=False,
    )
```

```python
import math

import jax
import jax.numpy as jnp
from jax import lax
from jax.experimental import pallas as pl
from jax.experimental.pallas import tpu as pltpu
from jax.sharding import PartitionSpec as P

inner_rate = 0.02
first_decay = 0.5
second_decay = 0.95
adam_eps = 1e-08
weight_decay = 0.1
outer_rate = 0.7
outer_mu = 0.9
mix_keep = 0.5

BF = jnp.bfloat16
F32 = jnp.float32

D = 4608
KVW = 1024
TOK = 512
UNIT = 288
HALF = 2304
REPLICAS = 16
MIB = 1024 * 1024

EVEN, ODD, WIDE = 0, 1, 2
PART = 96
QUAD = 4 * PART
PARTS = range(3)
ORDERS = ((EVEN, ODD, WIDE), (ODD, WIDE, EVEN), (WIDE, EVEN, ODD))
FLIP = {EVEN: 2, ODD: 6, WIDE: 8}
SWAP_LAST = [(i, i ^ 1) for i in range(16)]
ALONG_Z = [list(range(0, 16, 2)), list(range(1, 16, 2))]


def chip_bit(chip, dim):
    x = chip % 4
    if dim == EVEN:
        return (x ^ (x // 2)) % 2
    if dim == ODD:
        return x // 2
    return chip // 4


def unit_order(part):
    one, two, three = ORDERS[part]
    return sorted(
        range(8), key=lambda chip: (chip_bit(chip, three), chip_bit(chip, two), chip_bit(chip, one))
    )


def own_bits():
    me = lax.axis_index("fsdp")
    core = me & 1
    x = (me >> 1) & 3
    bits = {EVEN: (x ^ (x >> 1)) & 1, ODD: x >> 1, WIDE: me >> 3}
    places = [[bits[dim] for dim in order] for order in ORDERS]
    return core.astype(jnp.int32), places


def flip(value, part, step):
    return lax.ppermute(value, "fsdp", [(i, i ^ FLIP[ORDERS[part][step]]) for i in range(16)])


def swap(value):
    return lax.ppermute(value, "fsdp", SWAP_LAST)


def params(mib):
    return pltpu.CompilerParams(vmem_limit_bytes=mib * MIB)


def cost(flops, nbytes):
    return pl.CostEstimate(flops=flops, bytes_accessed=nbytes, transcendentals=0)


def pack_kernel(core_ref, rows_ref, out_ref):
    rows = rows_ref[...]

    def packed(core):
        pieces = []
        for part in PARTS:
            for chip in unit_order(part):
                at = 2 * UNIT * chip + UNIT * core + PART * part
                pieces.append(rows[:, at : at + PART])
        return jnp.concatenate(pieces, axis=1)

    @pl.when(core_ref[0] == 0)
    def _():
        out_ref[...] = packed(0)

    @pl.when(core_ref[0] == 1)
    def _():
        out_ref[...] = packed(1)


def pack(core, rows):
    tile = 256
    return pl.pallas_call(
        pack_kernel,
        grid_spec=pltpu.PrefetchScalarGridSpec(
            num_scalar_prefetch=1,
            grid=(TOK // tile,),
            in_specs=[pl.BlockSpec((tile, D), lambda i, s: (i, 0))],
            out_specs=pl.BlockSpec((tile, HALF), lambda i, s: (i, 0)),
        ),
        out_shape=jax.ShapeDtypeStruct((TOK, HALF), BF),
        compiler_params=params(14),
        cost_estimate=cost(0, 3 * TOK * D),
        name="pack",
    )(core, rows)


def turn_kernel(rows_ref, out_ref):
    out_ref[...] = rows_ref[...].T


def turn(rows):
    tile = 768
    return pl.pallas_call(
        turn_kernel,
        grid=(HALF // tile,),
        in_specs=[pl.BlockSpec((TOK, tile), lambda i: (0, i))],
        out_specs=pl.BlockSpec((tile, TOK), lambda i: (i, 0)),
        out_shape=jax.ShapeDtypeStruct((HALF, TOK), BF),
        compiler_params=params(8),
        cost_estimate=cost(0, 4 * TOK * HALF),
        name="turn",
    )(rows)


def dot(a, b):
    return jnp.dot(a, b, preferred_element_type=F32)


def product(refs):
    return sum(dot(refs[part][...], refs[3 + part][...]) for part in PARTS)


def project_near_kernel(at_ref, *refs):
    refs[-1][...] = product(refs)


def project_far_kernel(at_ref, *refs):
    refs[-1][...] = ((refs[-2][...] + product(refs)) * (1.0 / math.sqrt(D))).astype(BF)


def whole(*shape):
    return pl.BlockSpec(shape, lambda i, s: (0,) * len(shape))


def project(at, rows, quads, acc=None):
    near = acc is None

    def piece(part):
        return pl.BlockSpec((TOK, QUAD), lambda i, s: (0, s[part]))

    return pl.pallas_call(
        project_near_kernel if near else project_far_kernel,
        grid_spec=pltpu.PrefetchScalarGridSpec(
            num_scalar_prefetch=1,
            grid=(1,),
            in_specs=[piece(part) for part in PARTS]
            + [whole(QUAD, KVW)] * 3
            + ([] if near else [whole(TOK, KVW)]),
            out_specs=whole(TOK, KVW),
        ),
        out_shape=jax.ShapeDtypeStruct((TOK, KVW), F32 if near else BF),
        compiler_params=params(16),
        cost_estimate=cost(2 * TOK * KVW * 3 * QUAD, 7 * MIB),
        name="project_near" if near else "project_far",
    )(at, rows, rows, rows, *quads, *([] if near else [acc]))


def grad_kernel(at_ref, a_ref, b_ref, ra_ref, rb_ref, out_ref):
    out_ref[...] = (dot(a_ref[...], ra_ref[...]) + dot(b_ref[...], rb_ref[...])).astype(
        out_ref.dtype
    )


def grad_block(at, part, turned, residuals, dtype):
    piece = pl.BlockSpec((QUAD, TOK), lambda i, s: (s[part], 0))
    return pl.pallas_call(
        grad_kernel,
        grid_spec=pltpu.PrefetchScalarGridSpec(
            num_scalar_prefetch=1,
            grid=(1,),
            in_specs=[piece, piece, whole(TOK, KVW), whole(TOK, KVW)],
            out_specs=whole(QUAD, KVW),
        ),
        out_shape=jax.ShapeDtypeStruct((QUAD, KVW), dtype),
        compiler_params=params(12),
        cost_estimate=cost(4 * QUAD * KVW * TOK, 5 * MIB),
        name="grad",
    )(at, *turned, *residuals)


def inner_kernel(*refs):
    stay, came = refs[0:3], refs[3:6]
    w_ref, m_ref, v_ref, g_ref, m_out, v_out, w_out, delta_out = refs[6:]
    for part in PARTS:
        rows = slice(PART * part, PART * part + PART)
        grad = stay[part][...] + came[part][...].astype(F32)
        grad = grad * (1.0 / math.sqrt(TOK * 16))
        first = first_decay * m_ref[rows] + (1.0 - first_decay) * grad
        second = second_decay * v_ref[rows] + (1.0 - second_decay) * grad * grad
        m_out[rows] = first
        v_out[rows] = second
        wide = w_ref[rows].astype(F32)
        weight = (
            wide - inner_rate * (first / (jnp.sqrt(second) + adam_eps) + weight_decay * wide)
        ).astype(BF)
        w_out[rows] = weight
        delta = (g_ref[rows] - weight.astype(F32)).astype(BF)
        for group in range(delta_out.shape[0]):
            delta_out[group, rows] = delta[:, 128 * group : 128 * group + 128]


def inner(stay, came, weight, first, second, base):
    tile = 512
    piece = pl.BlockSpec((PART, tile), lambda i: (0, i))
    block = pl.BlockSpec((UNIT, tile), lambda i: (0, i))
    wide = jax.ShapeDtypeStruct((UNIT, KVW), F32)
    return pl.pallas_call(
        inner_kernel,
        grid=(KVW // tile,),
        in_specs=[piece] * 6 + [block] * 4,
        out_specs=[block, block, block, pl.BlockSpec((tile // 128, UNIT, 128), lambda i: (i, 0, 0))],
        out_shape=[
            wide,
            wide,
            jax.ShapeDtypeStruct((UNIT, KVW), BF),
            jax.ShapeDtypeStruct((KVW // 128, UNIT, 128), BF),
        ],
        compiler_params=params(16),
        cost_estimate=cost(20 * UNIT * KVW, 9 * MIB),
        name="inner",
    )(*stay, *came, weight, first, second, base)


def total_kernel(parts_ref, out_ref):
    out_ref[...] = jnp.sum(parts_ref[...].astype(F32), axis=0).astype(BF)


def totals(parts):
    return pl.pallas_call(
        total_kernel,
        out_shape=jax.ShapeDtypeStruct(parts.shape[1:], BF),
        compiler_params=params(8),
        cost_estimate=cost(0, MIB),
        name="totals",
    )(parts)


def replica_mean(delta):
    pieces = lax.all_to_all(delta, "replica", 0, 0, axis_index_groups=ALONG_Z)
    part = totals(pieces)
    other = lax.ppermute(part, "replica", SWAP_LAST)
    mean = ((part.astype(F32) + other.astype(F32)) * (1.0 / REPLICAS)).astype(BF)
    pieces = jnp.broadcast_to(mean[None], pieces.shape)
    return lax.all_to_all(pieces, "replica", 0, 0, axis_index_groups=ALONG_Z)


def outer_kernel(mean_ref, w_ref, g_ref, o_ref, local_out, global_out, momentum_out):
    groups = mean_ref.shape[0]
    mean = jnp.concatenate([mean_ref[group] for group in range(groups)], axis=1).astype(F32)
    momentum = outer_mu * o_ref[...] + mean
    base = g_ref[...] - outer_rate * (mean + outer_mu * momentum)
    momentum_out[...] = momentum
    global_out[...] = base
    local_out[...] = (mix_keep * w_ref[...].astype(F32) + (1.0 - mix_keep) * base).astype(BF)


def outer(mean, weight, base, momentum):
    tile = 512
    block = pl.BlockSpec((UNIT, tile), lambda i: (0, i))
    wide = jax.ShapeDtypeStruct((UNIT, KVW), F32)
    return pl.pallas_call(
        outer_kernel,
        grid=(KVW // tile,),
        in_specs=[pl.BlockSpec((tile // 128, UNIT, 128), lambda i: (i, 0, 0)), block, block, block],
        out_specs=[block, block, block],
        out_shape=[jax.ShapeDtypeStruct((UNIT, KVW), BF), wide, wide],
        compiler_params=params(16),
        cost_estimate=cost(8 * UNIT * KVW, 7 * MIB),
        name="outer",
    )(mean, weight, base, momentum)


def ordered(own_first, own, other):
    return jnp.where(
        own_first, jnp.concatenate([own, other], axis=0), jnp.concatenate([other, own], axis=0)
    )


def half_at(value, first):
    size = value.shape[0] // 2
    return jnp.where(first, value[:size], value[size:])


def local(
    tokens, targets, local_weights, first_moment, second_moment, global_weights, outer_momentum
):
    rows = tokens[0]
    wanted = targets[0]
    weight = local_weights[0]
    core, places = own_bits()
    near_at = jnp.stack([2 * part + places[part][2] for part in PARTS]).astype(jnp.int32)
    far_at = jnp.stack([2 * part + 1 - places[part][2] for part in PARTS]).astype(jnp.int32)

    lower = [[place == 0 for place in row] for row in places]
    upper = [[place != 0 for place in row] for row in places]
    core, near_at, far_at, lower, upper, weight, rows = lax.optimization_barrier(
        (core.reshape(1), near_at, far_at, lower, upper, weight, rows)
    )

    rows_other = swap(rows)
    held = [weight[PART * part : PART * part + PART] for part in PARTS]
    came = [flip(held[part], part, 0) for part in PARTS]
    held = [ordered(lower[part][0], held[part], came[part]) for part in PARTS]
    rows, held = lax.optimization_barrier((rows, held))
    came = [flip(held[part], part, 1) for part in PARTS]
    kept = pack(core, rows)
    came, kept, rows_other = lax.optimization_barrier((came, kept, rows_other))
    held = [ordered(lower[part][1], held[part], came[part]) for part in PARTS]
    far = [flip(held[part], part, 2) for part in PARTS]

    received = pack(core, rows_other)
    wanted_other = swap(wanted)
    turned = (turn(kept), turn(received))
    near_kept = project(near_at, kept, held)
    near_received = project(near_at, received, held)
    far, near_kept, near_received, turned, wanted_other = lax.optimization_barrier(
        (far, near_kept, near_received, turned, wanted_other)
    )
    own_received = project(far_at, received, far, near_received)
    cross_kept = swap(own_received)
    own_kept = project(far_at, kept, far, near_kept)
    cross_received = swap(own_kept)
    residuals = (
        (own_kept.astype(F32) + cross_kept.astype(F32) - wanted.astype(F32)).astype(BF),
        (own_received.astype(F32) + cross_received.astype(F32) - wanted_other.astype(F32)).astype(
            BF
        ),
    )

    came = [flip(grad_block(far_at, part, turned, residuals, BF), part, 2) for part in PARTS]
    sums = [grad_block(near_at, part, turned, residuals, F32) for part in PARTS]
    for step in (1, 0):
        sums = [sums[part] + came[part].astype(F32) for part in PARTS]
        came = [
            flip(half_at(sums[part], upper[part][step]).astype(BF), part, step)
            for part in PARTS
        ]
        sums = [half_at(sums[part], lower[part][step]) for part in PARTS]

    first, second, weight, delta = inner(
        sums, came, weight, first_moment[0], second_moment[0], global_weights
    )
    mean = replica_mean(delta)
    new_local, new_global, new_momentum = outer(mean, weight, global_weights, outer_momentum)
    return (new_local[None], first[None], second[None], new_global, new_momentum)


def solution(mesh):
    return jax.shard_map(
        local,
        mesh=mesh,
        in_specs=(
            P("replica", "fsdp", None),
            P("replica", "fsdp", None),
            P("replica", "fsdp", None),
            P("replica", "fsdp", None),
            P("replica", "fsdp", None),
            P("fsdp", None),
            P("fsdp", None),
        ),
        out_specs=(
            P("replica", "fsdp", None),
            P("replica", "fsdp", None),
            P("replica", "fsdp", None),
            P("fsdp", None),
            P("fsdp", None),
        ),
        check_vma=False,
    )
```

```python
import math

import jax
import jax.numpy as jnp
from jax import lax
from jax.experimental import pallas as pl
from jax.experimental.pallas import tpu as pltpu
from jax.sharding import PartitionSpec as P

inner_rate = 0.02
first_decay = 0.5
second_decay = 0.95
adam_eps = 1e-08
weight_decay = 0.1
outer_rate = 0.7
outer_mu = 0.9
mix_keep = 0.5

BF = jnp.bfloat16
F32 = jnp.float32

D = 4608
KVW = 1024
TOK = 512
UNIT = 288
HALF = 2304
REPLICAS = 16
MIB = 1024 * 1024

EVEN, ODD, WIDE = 1, 2, 4
ORDER = (0, EVEN, ODD, WIDE, EVEN | ODD, ODD | WIDE, EVEN | WIDE, EVEN | ODD | WIDE)
CHIP_FLIP = {EVEN: 1, ODD: 3, WIDE: 4}
PART = 96
PAIR = 2 * PART
QUAD = 4 * PART
PARTS = range(3)
ORDERS = ((ODD, WIDE, EVEN), (EVEN, ODD, WIDE), (WIDE, EVEN, ODD))
FIRST = 4 * UNIT
SWAP_LAST = [(i, i ^ 1) for i in range(16)]
ALONG_Z = [list(range(0, 16, 2)), list(range(1, 16, 2))]


SENT = {dim: [] for dim in (EVEN, ODD, WIDE)}
for part_of, (one, two, three) in enumerate(ORDERS):
    SENT[two].append((one, part_of))
    SENT[three] += [(one, part_of), (two, part_of)]


def chip_mask(away):
    mask = 0
    for dim, flipped in CHIP_FLIP.items():
        if away & dim:
            mask ^= flipped
    return mask


def rows_of(away, part):
    at = UNIT * ORDER.index(away) + PART * part
    return slice(at, at + PART)


def flip(value, dim):
    return lax.ppermute(value, "fsdp", [(i, i ^ (2 * CHIP_FLIP[dim])) for i in range(16)])


def swap(value):
    return lax.ppermute(value, "fsdp", SWAP_LAST)


def params(mib):
    return pltpu.CompilerParams(vmem_limit_bytes=mib * MIB)


def cost(flops, nbytes):
    return pl.CostEstimate(flops=flops, bytes_accessed=nbytes, transcendentals=0)


def turn_kernel(at_ref, rows_ref, out_ref, wide_ref):
    step = pl.program_id(0)
    wide_ref[...] = rows_ref[...].T
    for side in range(2):
        source = pl.multiple_of(at_ref[8] + 2 * UNIT * side, 32)
        target = pl.multiple_of(at_ref[2 * step + side], 32)
        out_ref[pl.ds(target, UNIT)] = wide_ref[pl.ds(source, UNIT)]


def turn(at, rows):
    return pl.pallas_call(
        turn_kernel,
        grid_spec=pltpu.PrefetchScalarGridSpec(
            num_scalar_prefetch=1,
            grid=(4,),
            in_specs=[pl.BlockSpec((TOK, 4 * UNIT), lambda i, s: (0, i))],
            out_specs=pl.BlockSpec((HALF, TOK), lambda i, s: (0, 0)),
            scratch_shapes=[pltpu.VMEM((4 * UNIT, TOK), BF)],
        ),
        out_shape=jax.ShapeDtypeStruct((HALF, TOK), BF),
        compiler_params=params(14),
        cost_estimate=cost(0, 3 * TOK * D),
        name="turn",
    )(at, rows)


def back_kernel(rows_ref, out_ref):
    out_ref[...] = rows_ref[...].T


def back(turned):
    tile = 768
    return pl.pallas_call(
        back_kernel,
        grid=(HALF // tile,),
        in_specs=[pl.BlockSpec((tile, TOK), lambda i: (i, 0))],
        out_specs=pl.BlockSpec((TOK, tile), lambda i: (0, i)),
        out_shape=jax.ShapeDtypeStruct((TOK, HALF), BF),
        compiler_params=params(8),
        cost_estimate=cost(0, 4 * TOK * HALF),
        name="back",
    )(turned)


def dot(a, b):
    return jnp.dot(a, b, preferred_element_type=F32)


def first_kernel(rows_ref, *refs):
    out_ref, block = refs[4:]
    for i in range(4):
        block[UNIT * i : UNIT * i + UNIT] = refs[i][...]
    out_ref[...] = dot(rows_ref[...], block[...])


def second_kernel(rows_ref, even, odd, wide, acc_ref, out_ref, block):
    came = {EVEN: even, ODD: odd, WIDE: wide}
    for dim in (EVEN, ODD, WIDE):
        for i, (away, part) in enumerate(SENT[dim]):
            at = rows_of(away | dim, part).start - FIRST
            block[at : at + PART] = came[dim][PART * i : PART * i + PART]
    used = 3 * UNIT
    block[used:] = jnp.zeros((block.shape[0] - used, KVW), BF)
    out_ref[...] = acc_ref[...] + dot(rows_ref[:, : block.shape[0]], block[...])


def third_kernel(rows_ref, even, odd, wide, acc_ref, out_ref, block):
    came = {EVEN: even, ODD: odd, WIDE: wide}
    block[:PART] = jnp.zeros((PART, KVW), BF)
    for part in PARTS:
        block[PART * (part + 1) : PART * (part + 2)] = came[ORDERS[part][2]][...]
    total = acc_ref[...] + dot(rows_ref[...], block[...])
    out_ref[...] = (total * (1.0 / math.sqrt(D))).astype(BF)


def project(kernel, rows, width, index, weights, acc=None):
    last = kernel is third_kernel
    extra = [] if acc is None else [acc]
    whole = pl.BlockSpec((TOK, KVW), lambda i: (0, 0))
    depth = {first_kernel: FIRST, second_kernel: 7 * 128, third_kernel: QUAD}[kernel]
    return pl.pallas_call(
        kernel,
        grid=(1,),
        in_specs=[pl.BlockSpec((TOK, width), lambda i: (0, index))]
        + [pl.BlockSpec(value.shape, lambda i: (0, 0)) for value in weights]
        + [whole] * len(extra),
        out_specs=whole,
        out_shape=jax.ShapeDtypeStruct((TOK, KVW), BF if last else F32),
        scratch_shapes=[pltpu.VMEM((depth, KVW), BF)],
        compiler_params=params(17),
        cost_estimate=cost(2 * TOK * KVW * depth, 7 * MIB),
        name=kernel.__name__,
    )(rows, *weights, *extra)


def grad_blocks(groups, turned, residuals, dtype):
    def kernel(one, two, one_res, two_res, *outs):
        for group, out in zip(groups, outs):
            total = None
            for ref, res in ((one, one_res), (two, two_res)):
                rows = jnp.concatenate([ref[rows_of(*unit)] for unit in group], axis=0)
                term = dot(rows, res[...])
                total = term if total is None else total + term
            out[...] = total.astype(out.dtype)

    sizes = [PART * len(group) for group in groups]
    here = pl.BlockSpec(memory_space=pltpu.VMEM)
    return pl.pallas_call(
        kernel,
        in_specs=[here] * 4,
        out_specs=[here] * len(groups),
        out_shape=[jax.ShapeDtypeStruct((size, KVW), dtype) for size in sizes],
        compiler_params=params(14),
        cost_estimate=cost(4 * sum(sizes) * KVW * TOK, 5 * MIB),
        name="grad",
    )(*turned, *residuals)


def inner_kernel(*refs):
    stay, came = refs[0:3], refs[3:6]
    w_ref, m_ref, v_ref, g_ref, m_out, v_out, w_out, delta_out = refs[6:]
    tile = m_out.shape[1]
    columns = pl.ds(pl.multiple_of(pl.program_id(0) * tile, tile), tile)
    for part in PARTS:
        rows = slice(PART * part, PART * part + PART)
        grad = stay[part][:, columns] + came[part][:, columns].astype(F32)
        grad = grad * (1.0 / math.sqrt(TOK * 16))
        first = first_decay * m_ref[rows, columns] + (1.0 - first_decay) * grad
        second = second_decay * v_ref[rows, columns] + (1.0 - second_decay) * grad * grad
        m_out[rows] = first
        v_out[rows] = second
        wide = w_ref[rows, columns].astype(F32)
        weight = (
            wide - inner_rate * (first / (jnp.sqrt(second) + adam_eps) + weight_decay * wide)
        ).astype(BF)
        w_out[rows] = weight
        delta = (g_ref[rows, columns] - weight.astype(F32)).astype(BF)
        for group in range(delta_out.shape[0]):
            delta_out[group, rows] = delta[:, 128 * group : 128 * group + 128]


def inner(stay, came, weight, first, second, base):
    tile = 512
    here = pl.BlockSpec(memory_space=pltpu.VMEM)
    block = pl.BlockSpec((UNIT, tile), lambda i: (0, i))
    wide = jax.ShapeDtypeStruct((UNIT, KVW), F32)
    return pl.pallas_call(
        inner_kernel,
        grid=(KVW // tile,),
        in_specs=[here] * 10,
        out_specs=[block, block, block, pl.BlockSpec((tile // 128, UNIT, 128), lambda i: (i, 0, 0))],
        out_shape=[
            wide,
            wide,
            jax.ShapeDtypeStruct((UNIT, KVW), BF),
            jax.ShapeDtypeStruct((KVW // 128, UNIT, 128), BF),
        ],
        compiler_params=params(16),
        cost_estimate=cost(20 * UNIT * KVW, 9 * MIB),
        name="inner",
    )(*stay, *came, weight, first, second, base)


def total_kernel(parts_ref, out_ref):
    out_ref[...] = jnp.sum(parts_ref[...].astype(F32), axis=0).astype(BF)


def totals(parts):
    return pl.pallas_call(
        total_kernel,
        out_shape=jax.ShapeDtypeStruct(parts.shape[1:], BF),
        compiler_params=params(8),
        cost_estimate=cost(0, MIB),
        name="totals",
    )(parts)


def replica_mean(delta):
    pieces = lax.all_to_all(delta, "replica", 0, 0, axis_index_groups=ALONG_Z)
    part = totals(pieces)
    other = lax.ppermute(part, "replica", SWAP_LAST)
    mean = ((part.astype(F32) + other.astype(F32)) * (1.0 / REPLICAS)).astype(BF)
    pieces = jnp.broadcast_to(mean[None], pieces.shape)
    return lax.all_to_all(pieces, "replica", 0, 0, axis_index_groups=ALONG_Z)


def outer_kernel(mean_ref, w_ref, g_ref, o_ref, local_out, global_out, momentum_out):
    tile = local_out.shape[1]
    columns = pl.ds(pl.multiple_of(pl.program_id(0) * tile, tile), tile)
    first = pl.program_id(0) * (tile // 128)
    mean = jnp.concatenate([mean_ref[first + i] for i in range(tile // 128)], axis=1).astype(F32)
    momentum = outer_mu * o_ref[:, columns] + mean
    base = g_ref[:, columns] - outer_rate * (mean + outer_mu * momentum)
    momentum_out[...] = momentum
    global_out[...] = base
    mixed = mix_keep * w_ref[:, columns].astype(F32) + (1.0 - mix_keep) * base
    local_out[...] = mixed.astype(BF)


def outer(mean, weight, base, momentum):
    tile = 512
    here = pl.BlockSpec(memory_space=pltpu.VMEM)
    block = pl.BlockSpec((UNIT, tile), lambda i: (0, i))
    wide = jax.ShapeDtypeStruct((UNIT, KVW), F32)
    return pl.pallas_call(
        outer_kernel,
        grid=(KVW // tile,),
        in_specs=[here] * 4,
        out_specs=[block, block, block],
        out_shape=[jax.ShapeDtypeStruct((UNIT, KVW), BF), wide, wide],
        compiler_params=params(16),
        cost_estimate=cost(8 * UNIT * KVW, 7 * MIB),
        name="outer",
    )(mean, weight, base, momentum)


def local(
    tokens, targets, local_weights, first_moment, second_moment, global_weights, outer_momentum
):
    rows = tokens[0]
    wanted = targets[0]
    weight = local_weights[0]
    me = lax.axis_index("fsdp").astype(jnp.int32)
    places = []
    for chip in range(8):
        place = jnp.int32(0)
        for i, away in enumerate(ORDER):
            place = jnp.where((me >> 1) ^ chip_mask(away) == chip, UNIT * i, place)
        places.append(place)
    at = jnp.stack([*places, UNIT * (me & 1)]).astype(jnp.int32)
    at, weight, rows = lax.optimization_barrier((at, weight, rows))

    rows_other = swap(rows)
    dims = (EVEN, ODD, WIDE)
    near = {dim: flip(weight, dim) for dim in dims}
    kept = turn(at, rows)
    kept_rows = back(kept)
    (near, kept, kept_rows, rows_other) = lax.optimization_barrier(
        (near, kept, kept_rows, rows_other)
    )
    second = {
        dim: flip(
            jnp.concatenate(
                [near[away][PART * part : PART * part + PART] for away, part in SENT[dim]], axis=0
            ),
            dim,
        )
        for dim in dims
    }
    wanted_other = swap(wanted)
    received = turn(at, rows_other)
    received_rows = back(received)
    first_weights = [weight, *(near[dim] for dim in dims)]
    sum_kept = project(first_kernel, kept_rows, FIRST, 0, first_weights)
    sum_received = project(first_kernel, received_rows, FIRST, 0, first_weights)
    second, sum_kept, sum_received = lax.optimization_barrier((second, sum_kept, sum_received))
    third = {}
    for part in PARTS:
        one, two, three = ORDERS[part]
        index = SENT[two].index((one, part))
        third[three] = flip(second[two][PART * index : PART * index + PART], three)
    second_weights = [second[dim] for dim in dims]
    sum_received = project(second_kernel, received_rows, FIRST, 1, second_weights, sum_received)
    sum_kept = project(second_kernel, kept_rows, FIRST, 1, second_weights, sum_kept)
    third, sum_kept, sum_received, wanted_other = lax.optimization_barrier(
        (third, sum_kept, sum_received, wanted_other)
    )
    turned = (kept, received)
    third_weights = [third[dim] for dim in dims]
    own_received = project(third_kernel, received_rows, QUAD, 5, third_weights, sum_received)
    cross_kept = swap(own_received)
    own_kept = project(third_kernel, kept_rows, QUAD, 5, third_weights, sum_kept)
    cross_received = swap(own_kept)
    residuals = (
        (own_kept.astype(F32) + cross_kept.astype(F32) - wanted.astype(F32)).astype(BF),
        (own_received.astype(F32) + cross_received.astype(F32) - wanted_other.astype(F32)).astype(
            BF
        ),
    )

    pass_on, keep = [], []
    for part in PARTS:
        one, two, three = ORDERS[part]
        pass_on.append([(two, part), (one | two, part)])
        keep.append([(0, part), (one, part)])

    def beyond(group, part):
        return [(away | ORDERS[part][2], part) for away, _ in group]

    (quad,) = grad_blocks(
        [beyond(pass_on[0], 0) + beyond(keep[0], 0)], turned, residuals, BF
    )
    quad = flip(quad, ORDERS[0][2])
    came, late = [], []
    for part in (1, 2):
        go, stay = grad_blocks(
            [beyond(pass_on[part], part), beyond(keep[part], part)], turned, residuals, BF
        )
        came.append(flip(go, ORDERS[part][2]))
        late.append(stay)
    late = [flip(late[part - 1], ORDERS[part][2]) for part in (1, 2)]
    came = [quad[:PAIR], *came]
    late = [quad[PAIR:], *late]
    sums = grad_blocks(pass_on, turned, residuals, F32)
    sent = [(sums[part] + came[part].astype(F32)).astype(BF) for part in PARTS]
    came = [flip(sent[part], ORDERS[part][1]) for part in PARTS]
    late, residuals = lax.optimization_barrier((late, residuals))
    sums = grad_blocks(keep, turned, residuals, F32)
    sums = [sums[part] + late[part].astype(F32) + came[part].astype(F32) for part in PARTS]
    came = [flip(sums[part][PART:].astype(BF), ORDERS[part][0]) for part in PARTS]
    sums = [sums[part][:PART] for part in PARTS]

    first, second, weight, delta = inner(
        sums, came, weight, first_moment[0], second_moment[0], global_weights
    )
    mean = replica_mean(delta)
    new_local, new_global, new_momentum = outer(mean, weight, global_weights, outer_momentum)
    return (new_local[None], first[None], second[None], new_global, new_momentum)


def solution(mesh):
    return jax.shard_map(
        local,
        mesh=mesh,
        in_specs=(
            P("replica", "fsdp", None),
            P("replica", "fsdp", None),
            P("replica", "fsdp", None),
            P("replica", "fsdp", None),
            P("replica", "fsdp", None),
            P("fsdp", None),
            P("fsdp", None),
        ),
        out_specs=(
            P("replica", "fsdp", None),
            P("replica", "fsdp", None),
            P("replica", "fsdp", None),
            P("fsdp", None),
            P("fsdp", None),
        ),
        check_vma=False,
    )
```

```python
import math

import jax
import jax.numpy as jnp
from jax import lax
from jax.experimental import pallas as pl
from jax.experimental.pallas import tpu as pltpu
from jax.sharding import PartitionSpec as P

inner_rate = 0.02
first_decay = 0.5
second_decay = 0.95
adam_eps = 1e-08
weight_decay = 0.1
outer_rate = 0.7
outer_mu = 0.9
mix_keep = 0.5

BF = jnp.bfloat16
F32 = jnp.float32

D = 4608
KVW = 1024
TOK = 512
UNIT = 288
HALF = 2304
REPLICAS = 16
MIB = 1024 * 1024

WIDE, EVEN, ODD = 1, 2, 4
ORDER = (0, WIDE, EVEN, ODD, EVEN | ODD, ODD | WIDE, EVEN | WIDE, EVEN | ODD | WIDE)
CHIP_FLIP = {WIDE: 4, EVEN: 1, ODD: 3}
PART = 96
PAIR = 2 * PART
QUAD = 4 * PART
PARTS = range(3)
ORDERS = ((WIDE, ODD, EVEN), (EVEN, WIDE, ODD), (ODD, EVEN, WIDE))
FIRST = 4 * UNIT
SWAP_LAST = [(i, i ^ 1) for i in range(16)]
ALONG_Z = [list(range(0, 16, 2)), list(range(1, 16, 2))]


SENT = {dim: [] for dim in (WIDE, EVEN, ODD)}
for part_of, (one, two, three) in enumerate(ORDERS):
    SENT[two].append((one, part_of))
    SENT[three] += [(one, part_of), (two, part_of)]


def chip_mask(away):
    mask = 0
    for dim, flipped in CHIP_FLIP.items():
        if away & dim:
            mask ^= flipped
    return mask


def rows_of(away, part):
    at = UNIT * ORDER.index(away) + PART * part
    return slice(at, at + PART)


def flip(value, dim):
    return lax.ppermute(value, "fsdp", [(i, i ^ (2 * CHIP_FLIP[dim])) for i in range(16)])


def swap(value):
    return lax.ppermute(value, "fsdp", SWAP_LAST)


def params(mib):
    return pltpu.CompilerParams(vmem_limit_bytes=mib * MIB)


def cost(flops, nbytes):
    return pl.CostEstimate(flops=flops, bytes_accessed=nbytes, transcendentals=0)


def turn_kernel(at_ref, rows_ref, out_ref, wide_ref):
    step = pl.program_id(0)
    wide_ref[...] = rows_ref[...].T
    for side in range(2):
        source = pl.multiple_of(at_ref[8] + 2 * UNIT * side, 32)
        target = pl.multiple_of(at_ref[2 * step + side], 32)
        out_ref[pl.ds(target, UNIT)] = wide_ref[pl.ds(source, UNIT)]


def turn(at, rows):
    return pl.pallas_call(
        turn_kernel,
        grid_spec=pltpu.PrefetchScalarGridSpec(
            num_scalar_prefetch=1,
            grid=(4,),
            in_specs=[pl.BlockSpec((TOK, 4 * UNIT), lambda i, s: (0, i))],
            out_specs=pl.BlockSpec((HALF, TOK), lambda i, s: (0, 0)),
            scratch_shapes=[pltpu.VMEM((4 * UNIT, TOK), BF)],
        ),
        out_shape=jax.ShapeDtypeStruct((HALF, TOK), BF),
        compiler_params=params(14),
        cost_estimate=cost(0, 3 * TOK * D),
        name="turn",
    )(at, rows)


def back_kernel(rows_ref, out_ref):
    out_ref[...] = rows_ref[...].T


def back(turned):
    tile = 768
    return pl.pallas_call(
        back_kernel,
        grid=(HALF // tile,),
        in_specs=[pl.BlockSpec((tile, TOK), lambda i: (i, 0))],
        out_specs=pl.BlockSpec((TOK, tile), lambda i: (0, i)),
        out_shape=jax.ShapeDtypeStruct((TOK, HALF), BF),
        compiler_params=params(8),
        cost_estimate=cost(0, 4 * TOK * HALF),
        name="back",
    )(turned)


def dot(a, b):
    return jnp.dot(a, b, preferred_element_type=F32)


def first_kernel(rows_ref, *refs):
    out_ref, block = refs[4:]
    for i in range(4):
        block[UNIT * i : UNIT * i + UNIT] = refs[i][...]
    out_ref[...] = dot(rows_ref[...], block[...])


def second_kernel(rows_ref, wide, even, odd, acc_ref, out_ref, block):
    came = {EVEN: even, ODD: odd, WIDE: wide}
    for dim in (WIDE, EVEN, ODD):
        for i, (away, part) in enumerate(SENT[dim]):
            at = rows_of(away | dim, part).start - FIRST
            block[at : at + PART] = came[dim][PART * i : PART * i + PART]
    used = 3 * UNIT
    block[used:] = jnp.zeros((block.shape[0] - used, KVW), BF)
    out_ref[...] = acc_ref[...] + dot(rows_ref[:, : block.shape[0]], block[...])


def third_kernel(rows_ref, wide, even, odd, acc_ref, out_ref, block):
    came = {EVEN: even, ODD: odd, WIDE: wide}
    block[:PART] = jnp.zeros((PART, KVW), BF)
    for part in PARTS:
        block[PART * (part + 1) : PART * (part + 2)] = came[ORDERS[part][2]][...]
    total = acc_ref[...] + dot(rows_ref[...], block[...])
    out_ref[...] = (total * (1.0 / math.sqrt(D))).astype(BF)


def project(kernel, rows, width, index, weights, acc=None):
    last = kernel is third_kernel
    extra = [] if acc is None else [acc]
    whole = pl.BlockSpec((TOK, KVW), lambda i: (0, 0))
    depth = {first_kernel: FIRST, second_kernel: 7 * 128, third_kernel: QUAD}[kernel]
    return pl.pallas_call(
        kernel,
        grid=(1,),
        in_specs=[pl.BlockSpec((TOK, width), lambda i: (0, index))]
        + [pl.BlockSpec(value.shape, lambda i: (0, 0)) for value in weights]
        + [whole] * len(extra),
        out_specs=whole,
        out_shape=jax.ShapeDtypeStruct((TOK, KVW), BF if last else F32),
        scratch_shapes=[pltpu.VMEM((depth, KVW), BF)],
        compiler_params=params(17),
        cost_estimate=cost(2 * TOK * KVW * depth, 7 * MIB),
        name=kernel.__name__,
    )(rows, *weights, *extra)


def grad_blocks(groups, turned, residuals, dtype):
    def kernel(one, two, one_res, two_res, *outs):
        for group, out in zip(groups, outs):
            total = None
            for ref, res in ((one, one_res), (two, two_res)):
                rows = jnp.concatenate([ref[rows_of(*unit)] for unit in group], axis=0)
                term = dot(rows, res[...])
                total = term if total is None else total + term
            out[...] = total.astype(out.dtype)

    sizes = [PART * len(group) for group in groups]
    here = pl.BlockSpec(memory_space=pltpu.VMEM)
    return pl.pallas_call(
        kernel,
        in_specs=[here] * 4,
        out_specs=[here] * len(groups),
        out_shape=[jax.ShapeDtypeStruct((size, KVW), dtype) for size in sizes],
        compiler_params=params(14),
        cost_estimate=cost(4 * sum(sizes) * KVW * TOK, 5 * MIB),
        name="grad",
    )(*turned, *residuals)


def inner_kernel(*refs):
    stay, came = refs[0:3], refs[3:6]
    w_ref, m_ref, v_ref, g_ref, m_out, v_out, w_out, delta_out = refs[6:]
    tile = m_out.shape[1]
    columns = pl.ds(pl.multiple_of(pl.program_id(0) * tile, tile), tile)
    for part in PARTS:
        rows = slice(PART * part, PART * part + PART)
        grad = stay[part][:, columns] + came[part][:, columns].astype(F32)
        grad = grad * (1.0 / math.sqrt(TOK * 16))
        first = first_decay * m_ref[rows, columns] + (1.0 - first_decay) * grad
        second = second_decay * v_ref[rows, columns] + (1.0 - second_decay) * grad * grad
        m_out[rows] = first
        v_out[rows] = second
        wide = w_ref[rows, columns].astype(F32)
        weight = (
            wide - inner_rate * (first / (jnp.sqrt(second) + adam_eps) + weight_decay * wide)
        ).astype(BF)
        w_out[rows] = weight
        delta = (g_ref[rows, columns] - weight.astype(F32)).astype(BF)
        for group in range(delta_out.shape[0]):
            delta_out[group, rows] = delta[:, 128 * group : 128 * group + 128]


def inner(stay, came, weight, first, second, base):
    tile = 512
    here = pl.BlockSpec(memory_space=pltpu.VMEM)
    block = pl.BlockSpec((UNIT, tile), lambda i: (0, i))
    wide = jax.ShapeDtypeStruct((UNIT, KVW), F32)
    return pl.pallas_call(
        inner_kernel,
        grid=(KVW // tile,),
        in_specs=[here] * 10,
        out_specs=[block, block, block, pl.BlockSpec((tile // 128, UNIT, 128), lambda i: (i, 0, 0))],
        out_shape=[
            wide,
            wide,
            jax.ShapeDtypeStruct((UNIT, KVW), BF),
            jax.ShapeDtypeStruct((KVW // 128, UNIT, 128), BF),
        ],
        compiler_params=params(16),
        cost_estimate=cost(20 * UNIT * KVW, 9 * MIB),
        name="inner",
    )(*stay, *came, weight, first, second, base)


def total_kernel(parts_ref, out_ref):
    out_ref[...] = jnp.sum(parts_ref[...].astype(F32), axis=0).astype(BF)


def totals(parts):
    return pl.pallas_call(
        total_kernel,
        out_shape=jax.ShapeDtypeStruct(parts.shape[1:], BF),
        compiler_params=params(8),
        cost_estimate=cost(0, MIB),
        name="totals",
    )(parts)


def replica_mean(delta):
    pieces = lax.all_to_all(delta, "replica", 0, 0, axis_index_groups=ALONG_Z)
    part = totals(pieces)
    other = lax.ppermute(part, "replica", SWAP_LAST)
    mean = ((part.astype(F32) + other.astype(F32)) * (1.0 / REPLICAS)).astype(BF)
    pieces = jnp.broadcast_to(mean[None], pieces.shape)
    return lax.all_to_all(pieces, "replica", 0, 0, axis_index_groups=ALONG_Z)


def outer_kernel(mean_ref, w_ref, g_ref, o_ref, local_out, global_out, momentum_out):
    tile = local_out.shape[1]
    columns = pl.ds(pl.multiple_of(pl.program_id(0) * tile, tile), tile)
    first = pl.program_id(0) * (tile // 128)
    mean = jnp.concatenate([mean_ref[first + i] for i in range(tile // 128)], axis=1).astype(F32)
    momentum = outer_mu * o_ref[:, columns] + mean
    base = g_ref[:, columns] - outer_rate * (mean + outer_mu * momentum)
    momentum_out[...] = momentum
    global_out[...] = base
    mixed = mix_keep * w_ref[:, columns].astype(F32) + (1.0 - mix_keep) * base
    local_out[...] = mixed.astype(BF)


def outer(mean, weight, base, momentum):
    tile = 512
    here = pl.BlockSpec(memory_space=pltpu.VMEM)
    block = pl.BlockSpec((UNIT, tile), lambda i: (0, i))
    wide = jax.ShapeDtypeStruct((UNIT, KVW), F32)
    return pl.pallas_call(
        outer_kernel,
        grid=(KVW // tile,),
        in_specs=[here] * 4,
        out_specs=[block, block, block],
        out_shape=[jax.ShapeDtypeStruct((UNIT, KVW), BF), wide, wide],
        compiler_params=params(16),
        cost_estimate=cost(8 * UNIT * KVW, 7 * MIB),
        name="outer",
    )(mean, weight, base, momentum)


def local(
    tokens, targets, local_weights, first_moment, second_moment, global_weights, outer_momentum
):
    rows = tokens[0]
    wanted = targets[0]
    weight = local_weights[0]
    me = lax.axis_index("fsdp").astype(jnp.int32)
    places = []
    for chip in range(8):
        place = jnp.int32(0)
        for i, away in enumerate(ORDER):
            place = jnp.where((me >> 1) ^ chip_mask(away) == chip, UNIT * i, place)
        places.append(place)
    at = jnp.stack([*places, UNIT * (me & 1)]).astype(jnp.int32)
    at, weight, rows = lax.optimization_barrier((at, weight, rows))

    rows_other = swap(rows)
    dims = (WIDE, EVEN, ODD)
    near = {dim: flip(weight, dim) for dim in dims}
    kept = turn(at, rows)
    kept_rows = back(kept)
    (near, kept, kept_rows, rows_other) = lax.optimization_barrier(
        (near, kept, kept_rows, rows_other)
    )
    second = {
        dim: flip(
            jnp.concatenate(
                [near[away][PART * part : PART * part + PART] for away, part in SENT[dim]], axis=0
            ),
            dim,
        )
        for dim in dims
    }
    wanted_other = swap(wanted)
    received = turn(at, rows_other)
    received_rows = back(received)
    first_weights = [weight, *(near[dim] for dim in dims)]
    sum_kept = project(first_kernel, kept_rows, FIRST, 0, first_weights)
    sum_received = project(first_kernel, received_rows, FIRST, 0, first_weights)
    second, sum_kept, sum_received = lax.optimization_barrier((second, sum_kept, sum_received))
    third = {}
    for part in PARTS:
        one, two, three = ORDERS[part]
        index = SENT[two].index((one, part))
        third[three] = flip(second[two][PART * index : PART * index + PART], three)
    second_weights = [second[dim] for dim in dims]
    sum_received = project(second_kernel, received_rows, FIRST, 1, second_weights, sum_received)
    sum_kept = project(second_kernel, kept_rows, FIRST, 1, second_weights, sum_kept)
    third, sum_kept, sum_received, wanted_other = lax.optimization_barrier(
        (third, sum_kept, sum_received, wanted_other)
    )
    turned = (kept, received)
    third_weights = [third[dim] for dim in dims]
    own_received = project(third_kernel, received_rows, QUAD, 5, third_weights, sum_received)
    cross_kept = swap(own_received)
    own_kept = project(third_kernel, kept_rows, QUAD, 5, third_weights, sum_kept)
    cross_received = swap(own_kept)
    residuals = (
        (own_kept.astype(F32) + cross_kept.astype(F32) - wanted.astype(F32)).astype(BF),
        (own_received.astype(F32) + cross_received.astype(F32) - wanted_other.astype(F32)).astype(
            BF
        ),
    )

    pass_on, keep = [], []
    for part in PARTS:
        one, two, three = ORDERS[part]
        pass_on.append([(two, part), (one | two, part)])
        keep.append([(0, part), (one, part)])

    def beyond(group, part):
        return [(away | ORDERS[part][2], part) for away, _ in group]

    (quad,) = grad_blocks(
        [beyond(pass_on[0], 0) + beyond(keep[0], 0)], turned, residuals, BF
    )
    quad = flip(quad, ORDERS[0][2])
    came, late = [], []
    for part in (1, 2):
        go, stay = grad_blocks(
            [beyond(pass_on[part], part), beyond(keep[part], part)], turned, residuals, BF
        )
        came.append(flip(go, ORDERS[part][2]))
        late.append(stay)
    late = [flip(late[part - 1], ORDERS[part][2]) for part in (1, 2)]
    came = [quad[:PAIR], *came]
    late = [quad[PAIR:], *late]
    sums = grad_blocks(pass_on, turned, residuals, F32)
    sent = [(sums[part] + came[part].astype(F32)).astype(BF) for part in PARTS]
    came = [flip(sent[part], ORDERS[part][1]) for part in PARTS]
    late, residuals = lax.optimization_barrier((late, residuals))
    sums = grad_blocks(keep, turned, residuals, F32)
    sums = [sums[part] + late[part].astype(F32) + came[part].astype(F32) for part in PARTS]
    came = [flip(sums[part][PART:].astype(BF), ORDERS[part][0]) for part in PARTS]
    sums = [sums[part][:PART] for part in PARTS]

    first, second, weight, delta = inner(
        sums, came, weight, first_moment[0], second_moment[0], global_weights
    )
    mean = replica_mean(delta)
    new_local, new_global, new_momentum = outer(mean, weight, global_weights, outer_momentum)
    return (new_local[None], first[None], second[None], new_global, new_momentum)


def solution(mesh):
    return jax.shard_map(
        local,
        mesh=mesh,
        in_specs=(
            P("replica", "fsdp", None),
            P("replica", "fsdp", None),
            P("replica", "fsdp", None),
            P("replica", "fsdp", None),
            P("replica", "fsdp", None),
            P("fsdp", None),
            P("fsdp", None),
        ),
        out_specs=(
            P("replica", "fsdp", None),
            P("replica", "fsdp", None),
            P("replica", "fsdp", None),
            P("fsdp", None),
            P("fsdp", None),
        ),
        check_vma=False,
    )
```
